32 devices in a mesh: wide: 8 (over y, x, core), narrow: 4 (over z).
Axes of the slice: x: 2, y: 2, z: 4, core: 2. Of those that a mesh axis runs over, the one named last changes fastest.
Arguments:
- queries: bfloat16 [16384, 768], P(('wide', 'narrow')), may hold values from -150 to 150
- documents: bfloat16 [1024, 768], P(('wide', 'narrow')), may hold values from -5 to 5
- positives: int32 [16384], P(('wide', 'narrow')), may hold values from 0 to 1023
Outputs:
- losses: float32 [16384], P(('wide', 'narrow'))
- query_grad: bfloat16 [16384, 768], P(('wide', 'narrow'))
The draws below stay inside these ranges and needn't reach their ends.
All inputs are finite; a program needn't handle non-finite values. Where the reference program divides by a largest or mean magnitude, that divisor is 1e-20 or more.
Results may differ from the reference program's by a relative error of at most 0.005.
Values may be sent and summed in bfloat16 or wider, within the bound.
No kernel may reach another device: no remote copies, remote signals or barrier semaphores. Data moves between devices by JAX's collectives and lax.ppermute only.
A program may use at most 64 MiB of HBM per device.

```python
import jax
import jax.numpy as jnp
from jax import lax

E = 768
QUERIES = 16384
DOCS = 1024


def base_documents(key):
    values = jax.random.normal(jax.random.fold_in(key, 11), (DOCS, E), jnp.float32)
    return jnp.clip(values, -5.0, 5.0)


def draw_documents(key, part):
    return base_documents(key).astype(jnp.bfloat16)


def draw_queries(key, part):
    values = jnp.clip(jax.random.normal(jax.random.fold_in(key, 12), (QUERIES, E), jnp.float32), -5.0, 5.0)
    return values.astype(jnp.bfloat16)


def set_ends(entries, stream_key, least, largest):
    longest = entries.shape.index(max(entries.shape))
    spots = []
    for shift in (0, 1):
        where = [jax.random.randint(jax.random.fold_in(stream_key, axis), (), 0, length) for axis, length in enumerate(entries.shape)]
        where[longest] = (where[longest] + shift) % entries.shape[longest]
        spots.append(tuple(where))
    return entries.at[spots[0]].set(least).at[spots[1]].set(largest)


def setup_inputs(seed: int = 0) -> dict:
    streams_of = jax.random.split(jax.random.key(seed), 4)
    return {
        "queries": draw_queries(jax.random.fold_in(streams_of[3], 71), 0),
        "documents": draw_documents(jax.random.fold_in(streams_of[3], 71), 0),
        "positives": set_ends(jax.random.randint(streams_of[2], (QUERIES,), 0, DOCS), jax.random.fold_in(streams_of[2], 1), 0, DOCS - 1).astype(jnp.int32),
    }


def reference(queries, documents, positives):
    temper = E ** -0.5
    doc_values = documents.astype(jnp.float32)
    scales = jnp.max(jnp.abs(doc_values), axis=1) + 1e-6
    codes = (doc_values / scales[:, None]).astype(jnp.bfloat16)
    qblock = min(512, QUERIES)
    count = QUERIES // qblock
    query_blocks = queries.reshape(count, qblock, E)
    pos_blocks = positives.reshape(count, qblock)
    column_ids = jnp.arange(DOCS, dtype=jnp.int32)

    def one_block(pair):
        rows, picks = pair
        raw = jnp.dot(rows, codes.T, preferred_element_type=jnp.float32)
        scores = raw * scales[None, :] * temper
        top = jnp.max(scores, axis=1)
        lse = top + jnp.log(jnp.sum(jnp.exp(scores - top[:, None]), axis=1))
        hit = column_ids[None, :] == picks[:, None]
        chosen = jnp.sum(jnp.where(hit, scores, 0.0), axis=1)
        probs = jnp.exp(scores - lse[:, None])
        weights = ((probs - hit.astype(jnp.float32)) * scales[None, :]).astype(jnp.bfloat16)
        grad = jnp.dot(weights, codes, preferred_element_type=jnp.float32) * temper
        return lse - chosen, grad.astype(jnp.bfloat16)

    losses, grads = lax.map(one_block, (query_blocks, pos_blocks))
    return losses.reshape(QUERIES), grads.reshape(QUERIES, E)
```

```python
import functools

import jax
import jax.numpy as jnp
from jax import lax
from jax.experimental import pallas as pl
from jax.experimental.pallas import tpu as pltpu
from jax.sharding import PartitionSpec as P

AXES = ("wide", "narrow")
NT = (((1,), (1,)), ((), ()))


def to_row(column):
    parts = []
    for start in range(0, column.shape[0], 128):
        piece = column[start : start + 128]
        size = piece.shape[0]
        r = lax.broadcasted_iota(jnp.int32, (size, size), 0)
        c = lax.broadcasted_iota(jnp.int32, (size, size), 1)
        parts.append(jnp.sum(jnp.where(r == c, piece, 0), axis=0, keepdims=True))
    return parts[0] if len(parts) == 1 else jnp.concatenate(parts, axis=1)


def kernel(n_chunks, block, spot_ref, q_ref, *refs):
    chunks = refs[:n_chunks]
    loss_ref, grad_ref, codes_ref, scales_ref, scores_ref = refs[n_chunks:]
    width = q_ref.shape[1]
    temper = width ** (-0.5)
    rows = q_ref.shape[0]
    size = chunks[0].shape[0]
    for i, chunk in enumerate(chunks):
        values = chunk[...].astype(jnp.float32)
        scale = jnp.max(jnp.abs(values), axis=1, keepdims=True) + 1e-06
        codes_ref[pl.ds(i * size, size), :] = (values / scale).astype(jnp.bfloat16)
        scales_ref[:, pl.ds(i * size, size)] = to_row(scale)
    docs = n_chunks * size
    scale_row = scales_ref[...]
    for start in range(0, rows, block):
        span = pl.ds(start, block)
        raw = lax.dot_general(
            q_ref[span, :], codes_ref[...], NT, preferred_element_type=jnp.float32
        )
        scores = raw * (scale_row * temper)
        hit = lax.broadcasted_iota(jnp.int32, (block, docs), 1) == spot_ref[span, :]
        top = jnp.max(scores, axis=1, keepdims=True)
        powers = jnp.exp(scores - top)
        total = jnp.sum(powers, axis=1, keepdims=True)
        chosen = jnp.sum(jnp.where(hit, scores, 0.0), axis=1, keepdims=True)
        loss_ref[:, span] = to_row(top + jnp.log(total) - chosen)
        probs = powers * (1.0 / total)
        weights = ((probs - jnp.where(hit, 1.0, 0.0)) * scale_row).astype(jnp.bfloat16)
        grad = jnp.dot(weights, codes_ref[...], preferred_element_type=jnp.float32)
        grad_ref[span, :] = (grad * temper).astype(jnp.bfloat16)


def shards(wide, narrow, queries, documents, positives):
    own = documents.shape[0]
    rows, width = queries.shape
    me = lax.axis_index("wide") * narrow + lax.axis_index("narrow")
    spots = (positives ^ (me * own)).reshape(rows, 1)

    def swap(array, axis, size, bits):
        return lax.ppermute(array, axis, [(i, i ^ bits) for i in range(size)])

    others = {k: swap(documents, "narrow", narrow, k) for k in reversed(range(1, narrow))}
    column = jnp.concatenate([documents] + [others[k] for k in range(1, narrow)], axis=0)
    held = {0: column}
    for k in reversed(range(2, wide, 2)):
        held[k] = swap(column, "wide", wide, k)
    for k in range(0, wide, 2):
        held[k + 1] = swap(held[k], "wide", wide, 1)
    docs = own * wide * narrow
    block = min(rows, 256)
    vmem = pl.BlockSpec(memory_space=pltpu.VMEM)
    limit = 8 * docs * width + 12 * rows * width + 12 * block * docs + 4 * 2**20
    limit = min(limit, 60 * 2**20)
    losses, grads = pl.pallas_call(
        functools.partial(kernel, wide, block),
        out_shape=(
            jax.ShapeDtypeStruct((1, rows), jnp.float32),
            jax.ShapeDtypeStruct((rows, width), jnp.bfloat16),
        ),
        in_specs=[vmem] * (2 + wide),
        out_specs=(vmem, vmem),
        scratch_shapes=[
            pltpu.VMEM((docs, width), jnp.bfloat16),
            pltpu.VMEM((1, docs), jnp.float32),
            pltpu.VMEM((8, 128), jnp.float32),
        ],
        compiler_params=pltpu.CompilerParams(vmem_limit_bytes=limit),
        cost_estimate=pl.CostEstimate(
            flops=4 * rows * docs * width,
            bytes_accessed=4 * rows * width + 2 * docs * width,
            transcendentals=rows * docs,
        ),
    )(spots, queries, *[held[k] for k in range(wide)])
    return losses.reshape(rows), grads


def solution(mesh):
    wide, narrow = mesh.shape["wide"], mesh.shape["narrow"]
    rows = P(AXES, None)
    return jax.shard_map(
        functools.partial(shards, wide, narrow),
        mesh=mesh,
        in_specs=(rows, rows, P(AXES)),
        out_specs=(P(AXES), rows),
        check_vma=False,
    )
```

```python
import functools

import jax
import jax.numpy as jnp
from jax import lax
from jax.experimental import pallas as pl
from jax.experimental.pallas import tpu as pltpu
from jax.sharding import PartitionSpec as P

AXES = ("wide", "narrow")
NT = (((1,), (1,)), ((), ()))
VMEM = pl.BlockSpec(memory_space=pltpu.VMEM)
HBM = pl.BlockSpec(memory_space=pltpu.HBM)


def to_row(column):
    parts = []
    for start in range(0, column.shape[0], 128):
        piece = column[start : start + 128]
        size = piece.shape[0]
        r = lax.broadcasted_iota(jnp.int32, (size, size), 0)
        c = lax.broadcasted_iota(jnp.int32, (size, size), 1)
        parts.append(jnp.sum(jnp.where(r == c, piece, 0), axis=0, keepdims=True))
    return parts[0] if len(parts) == 1 else jnp.concatenate(parts, axis=1)


def encode(chunks, codes_ref, scales_ref):
    group, start = [], 0
    for chunk in chunks:
        group.append(chunk[...].astype(jnp.float32))
        size = sum(part.shape[0] for part in group)
        if size % 128 and chunk is not chunks[-1]:
            continue
        values = group[0] if len(group) == 1 else jnp.concatenate(group, axis=0)
        scale = jnp.max(jnp.abs(values), axis=1, keepdims=True) + 1e-06
        codes_ref[pl.ds(start, size), :] = (values / scale).astype(jnp.bfloat16)
        scales_ref[:, pl.ds(start, size)] = to_row(scale)
        group, start = [], start + size


def ids_row(bases, own):
    rows = []
    size = max(own, 128)
    lane = lax.broadcasted_iota(jnp.int32, (1, size), 1)
    for start in range(0, len(bases), size // own):
        group = bases[start : start + size // own]
        shift = jnp.full((1, size), group[0], jnp.int32)
        for i, base in enumerate(group[1:], 1):
            shift = jnp.where(lane >= i * own, base - i * own, shift)
        rows.append((lane + shift)[:, : len(group) * own])
    return rows[0] if len(rows) == 1 else jnp.concatenate(rows, axis=1)


def softmax_part(scores, hit):
    top = jnp.max(scores, axis=1, keepdims=True)
    powers = jnp.exp(scores - top)
    total = jnp.sum(powers, axis=1, keepdims=True)
    chosen = jnp.sum(jnp.where(hit, scores, 0.0), axis=1, keepdims=True)
    return top, powers, total, chosen


def product(q, codes):
    return lax.dot_general(q, codes, NT, preferred_element_type=jnp.float32)


def load_kernel(narrow, own, positives_hbm, queries_hbm, spot_ref, q_ref, positives_ref, sem):
    fetch = pltpu.make_async_copy(positives_hbm, positives_ref, sem.at[0])
    fetch.start()
    copy = pltpu.make_async_copy(queries_hbm, q_ref, sem.at[1])
    copy.start()
    fetch.wait()
    me = lax.axis_index("wide") * narrow + lax.axis_index("narrow")
    local = (positives_ref[...] ^ (me * own)).astype(jnp.float32)
    for start in range(0, local.shape[1], 128):
        piece = local[:, start : start + 128]
        size = piece.shape[1]
        r = lax.broadcasted_iota(jnp.int32, (size, size), 0)
        c = lax.broadcasted_iota(jnp.int32, (size, size), 1)
        spot = jnp.sum(jnp.where(r == c, piece, 0.0), axis=1, keepdims=True)
        spot_ref[pl.ds(start, size), :] = spot.astype(jnp.int32)
    copy.wait()


def early_kernel(bases, own, block, spot_ref, q_ref, *refs):
    chunks = refs[:-6]
    codes_ref, scales_ref, powers_ref, top_ref, total_ref, chosen_ref = refs[-6:]
    rows, width = q_ref.shape
    temper = width ** (-0.5)
    encode(chunks, codes_ref, scales_ref)
    ids = ids_row(bases, own)
    for start in range(0, rows, block):
        span = pl.ds(start, block)
        scores = product(q_ref[span, :], codes_ref[...]) * (scales_ref[...] * temper)
        top, powers, total, chosen = softmax_part(scores, ids == spot_ref[span, :])
        powers_ref[span, :] = powers
        top_ref[span, :] = top
        total_ref[span, :] = total
        chosen_ref[span, :] = chosen


def late_kernel(bases, own, block, spot_ref, q_ref, *refs):
    states = [refs[6 * i : 6 * i + 6] for i in range(len(bases) - 1)]
    chunks = refs[6 * len(states) : -9]
    loss_hbm, grad_hbm, codes_ref, late_scales_ref, weights_ref, loss_ref, grad_ref, sem, loss_sem = refs[-9:]
    rows, width = q_ref.shape
    temper = width ** (-0.5)
    n_late = len(bases[-1]) * own
    n_early = codes_ref.shape[0] - n_late
    late_codes_ref = codes_ref.at[pl.ds(n_early, n_late), :]
    encode(chunks, late_codes_ref, late_scales_ref)
    places = []
    for state in states:
        size = state[0].shape[0]
        places.append(pl.ds(sum(place.size for place in places), size))
        codes_ref[places[-1], :] = state[0][...]
    late_scales = late_scales_ref[...]
    ids = [ids_row(part, own) for part in bases]

    def weigh(start):
        span = pl.ds(start, block)
        spots = spot_ref[span, :]
        scores = product(q_ref[span, :], late_codes_ref[...]) * (late_scales * temper)
        late_hit = ids[-1] == spots
        late_top, late_powers, late_total, chosen = softmax_part(scores, late_hit)
        top = late_top
        for state in states:
            top = jnp.maximum(top, state[3][span, :])
        late_share = jnp.exp(late_top - top)
        shares = [jnp.exp(state[3][span, :] - top) for state in states]
        total = late_total * late_share
        for state, share in zip(states, shares):
            total += state[4][span, :] * share
            chosen += state[5][span, :]
        loss_ref[:, span] = to_row(top + jnp.log(total) - chosen)
        for state, share, place, part in zip(states, shares, places, ids):
            probs = state[2][span, :] * (share / total)
            weights = (probs - jnp.where(part == spots, 1.0, 0.0)) * state[1][...]
            weights_ref[span, place] = weights.astype(jnp.bfloat16)
        probs = late_powers * (late_share / total)
        weights = (probs - jnp.where(late_hit, 1.0, 0.0)) * late_scales
        weights_ref[span, pl.ds(n_early, n_late)] = weights.astype(jnp.bfloat16)

    starts = range(0, rows, block)
    for start in starts:
        weigh(start)
    copies = [pltpu.make_async_copy(loss_ref, loss_hbm, loss_sem)]
    copies[0].start()
    for i, start in enumerate(starts):
        span = pl.ds(start, block)
        grad = jnp.dot(weights_ref[span, :], codes_ref[...], preferred_element_type=jnp.float32)
        grad_ref[span, :] = (grad * temper).astype(jnp.bfloat16)
        copy = pltpu.make_async_copy(grad_ref.at[span, :], grad_hbm.at[span, :], sem.at[i])
        copy.start()
        copies.append(copy)
    for copy in copies:
        copy.wait()


def shards(wide, narrow, queries, documents, positives):
    own = documents.shape[0]
    rows, width = queries.shape
    f32, bf16 = jnp.float32, jnp.bfloat16
    barrier = lax.optimization_barrier
    block = min(rows, 256)
    far = range(2, wide, 2)

    def swap(array, axis, bits):
        size = wide if axis == "wide" else narrow
        return lax.ppermute(array, axis, [(i, i ^ bits) for i in range(size)])

    def params(docs, kept):
        held = 6 * docs * width + 8 * rows * width + 4 * rows * (kept + 512) + 12 * block * docs
        return dict(
            compiler_params=pltpu.CompilerParams(
                vmem_limit_bytes=min(held + 4 * 2**20, 60 * 2**20)
            ),
            cost_estimate=pl.CostEstimate(flops=rows, bytes_accessed=rows, transcendentals=0),
        )

    def load(positives, queries):
        return pl.pallas_call(
            functools.partial(load_kernel, narrow, own),
            out_shape=(
                jax.ShapeDtypeStruct((rows, 1), jnp.int32),
                jax.ShapeDtypeStruct((rows, width), bf16),
            ),
            in_specs=[HBM, HBM],
            out_specs=(VMEM, VMEM),
            scratch_shapes=[pltpu.VMEM((1, rows), jnp.int32), pltpu.SemaphoreType.DMA((2,))],
            **params(0, 0),
        )(positives.reshape(1, rows), queries)

    def bases_of(distances):
        return [(k * narrow + n) * own for k in distances for n in range(narrow)]

    def score(spots, loaded, distances, chunks):
        docs = len(chunks) * own * narrow
        column = jax.ShapeDtypeStruct((rows, 1), f32)
        return pl.pallas_call(
            functools.partial(early_kernel, bases_of(distances), own, block),
            out_shape=(
                jax.ShapeDtypeStruct((docs, width), bf16),
                jax.ShapeDtypeStruct((1, docs), f32),
                jax.ShapeDtypeStruct((rows, docs), f32),
                column,
                column,
                column,
            ),
            in_specs=[VMEM] * (2 + len(chunks)),
            out_specs=(VMEM,) * 6,
            **params(docs, docs),
        )(spots, loaded, *chunks)

    shard = {k: swap(documents, "narrow", k) for k in reversed(range(1, narrow))}
    column = jnp.concatenate([documents] + [shard[k] for k in range(1, narrow)], axis=0)
    held = {k: swap(column, "wide", k) for k in reversed(far)}
    column, positives, queries = barrier((column, positives, queries))
    spots, loaded = load(positives, queries)
    held[0] = column
    spots, loaded, held = barrier((spots, loaded, held))
    mine = range(0, wide, 2)
    middle = score(spots, loaded, mine, [held[k] for k in mine])
    mirrored = [swap(held[k], "wide", 1) for k in mine]
    docs = own * narrow * wide
    bases = [bases_of(mine), bases_of([k ^ 1 for k in mine])]
    n_late = len(bases[-1]) * own
    losses, grads = pl.pallas_call(
        functools.partial(late_kernel, bases, own, block),
        out_shape=(
            jax.ShapeDtypeStruct((1, rows), f32),
            jax.ShapeDtypeStruct((rows, width), bf16),
        ),
        in_specs=[VMEM] * (2 + len(middle) + len(mirrored)),
        out_specs=(HBM, HBM),
        scratch_shapes=[
            pltpu.VMEM((docs, width), bf16),
            pltpu.VMEM((1, n_late), f32),
            pltpu.VMEM((rows, docs), bf16),
            pltpu.VMEM((1, rows), f32),
            pltpu.VMEM((rows, width), bf16),
            pltpu.SemaphoreType.DMA((rows // block,)),
            pltpu.SemaphoreType.DMA(()),
        ],
        **params(docs, docs),
    )(spots, loaded, *middle, *mirrored)
    return losses.reshape(rows), grads


def solution(mesh):
    wide, narrow = mesh.shape["wide"], mesh.shape["narrow"]
    rows = P(AXES, None)
    return jax.shard_map(
        functools.partial(shards, wide, narrow),
        mesh=mesh,
        in_specs=(rows, rows, P(AXES)),
        out_specs=(P(AXES), rows),
        check_vma=False,
    )
```

```python
import functools

import jax
import jax.numpy as jnp
from jax import lax
from jax.experimental import pallas as pl
from jax.experimental.pallas import tpu as pltpu
from jax.sharding import PartitionSpec as P

AXES = ("wide", "narrow")
NT = (((1,), (1,)), ((), ()))
VMEM = pl.BlockSpec(memory_space=pltpu.VMEM)
HBM = pl.BlockSpec(memory_space=pltpu.HBM)


def to_row(column):
    parts = []
    for start in range(0, column.shape[0], 128):
        piece = column[start : start + 128]
        size = piece.shape[0]
        r = lax.broadcasted_iota(jnp.int32, (size, size), 0)
        c = lax.broadcasted_iota(jnp.int32, (size, size), 1)
        parts.append(jnp.sum(jnp.where(r == c, piece, 0), axis=0, keepdims=True))
    return parts[0] if len(parts) == 1 else jnp.concatenate(parts, axis=1)


def encode(chunks, codes_ref, scales_ref):
    group, start = [], 0
    for chunk in chunks:
        group.append(chunk[...].astype(jnp.float32))
        size = sum(part.shape[0] for part in group)
        if size % 128 and chunk is not chunks[-1]:
            continue
        values = group[0] if len(group) == 1 else jnp.concatenate(group, axis=0)
        scale = jnp.max(jnp.abs(values), axis=1, keepdims=True) + 1e-06
        codes_ref[pl.ds(start, size), :] = (values / scale).astype(jnp.bfloat16)
        scales_ref[:, pl.ds(start, size)] = to_row(scale)
        group, start = [], start + size


def ids_row(bases, own):
    rows = []
    size = max(own, 128)
    lane = lax.broadcasted_iota(jnp.int32, (1, size), 1)
    for start in range(0, len(bases), size // own):
        group = bases[start : start + size // own]
        shift = jnp.full((1, size), group[0], jnp.int32)
        for i, base in enumerate(group[1:], 1):
            shift = jnp.where(lane >= i * own, base - i * own, shift)
        rows.append((lane + shift)[:, : len(group) * own])
    return rows[0] if len(rows) == 1 else jnp.concatenate(rows, axis=1)


def softmax_part(scores, hit):
    top = jnp.max(scores, axis=1, keepdims=True)
    powers = jnp.exp(scores - top)
    total = jnp.sum(powers, axis=1, keepdims=True)
    chosen = jnp.sum(jnp.where(hit, scores, 0.0), axis=1, keepdims=True)
    return top, powers, total, chosen


def product(q, codes):
    return lax.dot_general(q, codes, NT, preferred_element_type=jnp.float32)


def load_kernel(narrow, own, positives_hbm, queries_hbm, spot_ref, q_ref, positives_ref, sem):
    fetch = pltpu.make_async_copy(positives_hbm, positives_ref, sem.at[0])
    fetch.start()
    copy = pltpu.make_async_copy(queries_hbm, q_ref, sem.at[1])
    copy.start()
    fetch.wait()
    me = lax.axis_index("wide") * narrow + lax.axis_index("narrow")
    local = (positives_ref[...] ^ (me * own)).astype(jnp.float32)
    for start in range(0, local.shape[1], 128):
        piece = local[:, start : start + 128]
        size = piece.shape[1]
        r = lax.broadcasted_iota(jnp.int32, (size, size), 0)
        c = lax.broadcasted_iota(jnp.int32, (size, size), 1)
        spot = jnp.sum(jnp.where(r == c, piece, 0.0), axis=1, keepdims=True)
        spot_ref[pl.ds(start, size), :] = spot.astype(jnp.int32)
    copy.wait()


def early_kernel(bases, own, block, spot_ref, q_ref, *refs):
    chunks = refs[:-6]
    codes_ref, scales_ref, powers_ref, top_ref, total_ref, chosen_ref = refs[-6:]
    rows, width = q_ref.shape
    temper = width ** (-0.5)
    encode(chunks, codes_ref, scales_ref)
    ids = ids_row(bases, own)
    for start in range(0, rows, block):
        span = pl.ds(start, block)
        scores = product(q_ref[span, :], codes_ref[...]) * (scales_ref[...] * temper)
        top, powers, total, chosen = softmax_part(scores, ids == spot_ref[span, :])
        powers_ref[span, :] = powers
        top_ref[span, :] = top
        total_ref[span, :] = total
        chosen_ref[span, :] = chosen


def late_kernel(bases, own, block, spot_ref, q_ref, *refs):
    states = [refs[6 * i : 6 * i + 6] for i in range(len(bases) - 1)]
    chunks = refs[6 * len(states) : -9]
    loss_hbm, grad_hbm, codes_ref, late_scales_ref, weights_ref, loss_ref, grad_ref, sem, loss_sem = refs[-9:]
    rows, width = q_ref.shape
    temper = width ** (-0.5)
    n_late = len(bases[-1]) * own
    n_early = codes_ref.shape[0] - n_late
    late_codes_ref = codes_ref.at[pl.ds(n_early, n_late), :]
    encode(chunks, late_codes_ref, late_scales_ref)
    places = []
    for state in states:
        size = state[0].shape[0]
        places.append(pl.ds(sum(place.size for place in places), size))
        codes_ref[places[-1], :] = state[0][...]
    late_scales = late_scales_ref[...]
    ids = [ids_row(part, own) for part in bases]

    def weigh(start):
        span = pl.ds(start, block)
        spots = spot_ref[span, :]
        scores = product(q_ref[span, :], late_codes_ref[...]) * (late_scales * temper)
        late_hit = ids[-1] == spots
        late_top, late_powers, late_total, chosen = softmax_part(scores, late_hit)
        top = late_top
        for state in states:
            top = jnp.maximum(top, state[3][span, :])
        late_share = jnp.exp(late_top - top)
        shares = [jnp.exp(state[3][span, :] - top) for state in states]
        total = late_total * late_share
        for state, share in zip(states, shares):
            total += state[4][span, :] * share
            chosen += state[5][span, :]
        loss_ref[:, span] = to_row(top + jnp.log(total) - chosen)
        for state, share, place, part in zip(states, shares, places, ids):
            probs = state[2][span, :] * (share / total)
            weights = (probs - jnp.where(part == spots, 1.0, 0.0)) * state[1][...]
            weights_ref[span, place] = weights.astype(jnp.bfloat16)
        probs = late_powers * (late_share / total)
        weights = (probs - jnp.where(late_hit, 1.0, 0.0)) * late_scales
        weights_ref[span, pl.ds(n_early, n_late)] = weights.astype(jnp.bfloat16)

    starts = range(0, rows, block)
    for start in starts:
        weigh(start)
    copies = [pltpu.make_async_copy(loss_ref, loss_hbm, loss_sem)]
    copies[0].start()
    for i, start in enumerate(starts):
        span = pl.ds(start, block)
        grad = jnp.dot(weights_ref[span, :], codes_ref[...], preferred_element_type=jnp.float32)
        grad_ref[span, :] = (grad * temper).astype(jnp.bfloat16)
        copy = pltpu.make_async_copy(grad_ref.at[span, :], grad_hbm.at[span, :], sem.at[i])
        copy.start()
        copies.append(copy)
    for copy in copies:
        copy.wait()


def shards(wide, narrow, queries, documents, positives):
    own = documents.shape[0]
    rows, width = queries.shape
    f32, bf16 = jnp.float32, jnp.bfloat16
    barrier = lax.optimization_barrier
    block = min(rows, 256)
    far = range(2, wide, 2)
    evens = list(range(0, narrow, 2))
    order = evens + [k ^ 1 for k in evens]

    def swap(array, axis, bits):
        size = wide if axis == "wide" else narrow
        return lax.ppermute(array, axis, [(i, i ^ bits) for i in range(size)])

    def params(docs, kept):
        held = 6 * docs * width + 8 * rows * width + 4 * rows * (kept + 512) + 12 * block * docs
        return dict(
            compiler_params=pltpu.CompilerParams(
                vmem_limit_bytes=min(held + 4 * 2**20, 60 * 2**20)
            ),
            cost_estimate=pl.CostEstimate(flops=rows, bytes_accessed=rows, transcendentals=0),
        )

    def load(positives, queries):
        return pl.pallas_call(
            functools.partial(load_kernel, narrow, own),
            out_shape=(
                jax.ShapeDtypeStruct((rows, 1), jnp.int32),
                jax.ShapeDtypeStruct((rows, width), bf16),
            ),
            in_specs=[HBM, HBM],
            out_specs=(VMEM, VMEM),
            scratch_shapes=[pltpu.VMEM((1, rows), jnp.int32), pltpu.SemaphoreType.DMA((2,))],
            **params(0, 0),
        )(positives.reshape(1, rows), queries)

    def bases_of(distances):
        return [(k * narrow + n) * own for k in distances for n in order]

    def score(spots, loaded, distances, chunks):
        docs = len(distances) * own * narrow
        column = jax.ShapeDtypeStruct((rows, 1), f32)
        return pl.pallas_call(
            functools.partial(early_kernel, bases_of(distances), own, block),
            out_shape=(
                jax.ShapeDtypeStruct((docs, width), bf16),
                jax.ShapeDtypeStruct((1, docs), f32),
                jax.ShapeDtypeStruct((rows, docs), f32),
                column,
                column,
                column,
            ),
            in_specs=[VMEM] * (2 + len(chunks)),
            out_specs=(VMEM,) * 6,
            **params(docs, docs),
        )(spots, loaded, *chunks)

    shard = {0: documents} | {k: swap(documents, "narrow", k) for k in evens[1:]}
    base = jnp.concatenate([shard[k] for k in evens], axis=0)
    firsts = {k: swap(base, "wide", k) for k in far if k & (k - 1)}
    other = swap(base, "narrow", 1)
    column = jnp.concatenate([base, other], axis=0)
    held = {}
    for k in far:
        if k & (k - 1) == 0:
            held[k] = [swap(column, "wide", k)]
        else:
            held[k] = [firsts[k], swap(firsts[k], "narrow", 1)]
    column, positives, queries = barrier((column, positives, queries))
    spots, loaded = load(positives, queries)
    held[0] = [column]
    spots, loaded, held = barrier((spots, loaded, held))
    mine = range(0, wide, 2)
    middle = score(spots, loaded, mine, [part for k in mine for part in held[k]])
    mirrored = [swap(part, "wide", 1) for k in mine for part in held[k]]
    docs = own * narrow * wide
    bases = [bases_of(mine), bases_of([k ^ 1 for k in mine])]
    n_late = len(bases[-1]) * own
    losses, grads = pl.pallas_call(
        functools.partial(late_kernel, bases, own, block),
        out_shape=(
            jax.ShapeDtypeStruct((1, rows), f32),
            jax.ShapeDtypeStruct((rows, width), bf16),
        ),
        in_specs=[VMEM] * (2 + len(middle) + len(mirrored)),
        out_specs=(HBM, HBM),
        scratch_shapes=[
            pltpu.VMEM((docs, width), bf16),
            pltpu.VMEM((1, n_late), f32),
            pltpu.VMEM((rows, docs), bf16),
            pltpu.VMEM((1, rows), f32),
            pltpu.VMEM((rows, width), bf16),
            pltpu.SemaphoreType.DMA((rows // block,)),
            pltpu.SemaphoreType.DMA(()),
        ],
        **params(docs, docs),
    )(spots, loaded, *middle, *mirrored)
    return losses.reshape(rows), grads


def solution(mesh):
    wide, narrow = mesh.shape["wide"], mesh.shape["narrow"]
    rows = P(AXES, None)
    return jax.shard_map(
        functools.partial(shards, wide, narrow),
        mesh=mesh,
        in_specs=(rows, rows, P(AXES)),
        out_specs=(P(AXES), rows),
        check_vma=False,
    )
```

```python
import functools

import jax
import jax.numpy as jnp
from jax import lax
from jax.experimental import pallas as pl
from jax.experimental.pallas import tpu as pltpu
from jax.sharding import PartitionSpec as P

AXES = ("wide", "narrow")
NT = (((1,), (1,)), ((), ()))
VMEM = pl.BlockSpec(memory_space=pltpu.VMEM)
HBM = pl.BlockSpec(memory_space=pltpu.HBM)


def to_row(column):
    parts = []
    for start in range(0, column.shape[0], 128):
        piece = column[start : start + 128]
        size = piece.shape[0]
        r = lax.broadcasted_iota(jnp.int32, (size, size), 0)
        c = lax.broadcasted_iota(jnp.int32, (size, size), 1)
        parts.append(jnp.sum(jnp.where(r == c, piece, 0), axis=0, keepdims=True))
    return parts[0] if len(parts) == 1 else jnp.concatenate(parts, axis=1)


def encode(chunks, codes_ref, scales_ref):
    group, start = [], 0
    for chunk in chunks:
        group.append(chunk[...].astype(jnp.float32))
        size = sum(part.shape[0] for part in group)
        if size % 128 and chunk is not chunks[-1]:
            continue
        values = group[0] if len(group) == 1 else jnp.concatenate(group, axis=0)
        scale = jnp.max(jnp.abs(values), axis=1, keepdims=True) + 1e-06
        codes_ref[pl.ds(start, size), :] = (values / scale).astype(jnp.bfloat16)
        scales_ref[:, pl.ds(start, size)] = to_row(scale)
        group, start = [], start + size


def ids_row(bases, own):
    rows = []
    size = max(own, 128)
    lane = lax.broadcasted_iota(jnp.int32, (1, size), 1)
    for start in range(0, len(bases), size // own):
        group = bases[start : start + size // own]
        shift = jnp.full((1, size), group[0], jnp.int32)
        for i, base in enumerate(group[1:], 1):
            shift = jnp.where(lane >= i * own, base - i * own, shift)
        rows.append((lane + shift)[:, : len(group) * own])
    return rows[0] if len(rows) == 1 else jnp.concatenate(rows, axis=1)


def softmax_part(scores, hit):
    top = jnp.max(scores, axis=1, keepdims=True)
    powers = jnp.exp(scores - top)
    total = jnp.sum(powers, axis=1, keepdims=True)
    chosen = jnp.sum(jnp.where(hit, scores, 0.0), axis=1, keepdims=True)
    return top, powers, total, chosen


def product(q, codes):
    return lax.dot_general(q, codes, NT, preferred_element_type=jnp.float32)


def load_kernel(narrow, own, positives_hbm, queries_hbm, spot_ref, q_ref, positives_ref, sem):
    fetch = pltpu.make_async_copy(positives_hbm, positives_ref, sem.at[0])
    fetch.start()
    copy = pltpu.make_async_copy(queries_hbm, q_ref, sem.at[1])
    copy.start()
    fetch.wait()
    me = lax.axis_index("wide") * narrow + lax.axis_index("narrow")
    local = (positives_ref[...] ^ (me * own)).astype(jnp.float32)
    for start in range(0, local.shape[1], 128):
        piece = local[:, start : start + 128]
        size = piece.shape[1]
        r = lax.broadcasted_iota(jnp.int32, (size, size), 0)
        c = lax.broadcasted_iota(jnp.int32, (size, size), 1)
        spot = jnp.sum(jnp.where(r == c, piece, 0.0), axis=1, keepdims=True)
        spot_ref[pl.ds(start, size), :] = spot.astype(jnp.int32)
    copy.wait()


def early_kernel(bases, own, block, spot_ref, q_ref, *refs):
    chunks = refs[:-6]
    codes_ref, scales_ref, powers_ref, top_ref, total_ref, chosen_ref = refs[-6:]
    rows, width = q_ref.shape
    temper = width ** (-0.5)
    encode(chunks, codes_ref, scales_ref)
    ids = ids_row(bases, own)
    for start in range(0, rows, block):
        span = pl.ds(start, block)
        scores = product(q_ref[span, :], codes_ref[...]) * (scales_ref[...] * temper)
        top, powers, total, chosen = softmax_part(scores, ids == spot_ref[span, :])
        powers_ref[span, :] = powers
        top_ref[span, :] = top
        total_ref[span, :] = total
        chosen_ref[span, :] = chosen


def late_kernel(bases, own, block, spot_ref, q_ref, *refs):
    states = [refs[6 * i : 6 * i + 6] for i in range(len(bases) - 1)]
    chunks = refs[6 * len(states) : -9]
    loss_hbm, grad_hbm, codes_ref, late_scales_ref, weights_ref, loss_ref, grad_ref, sem, loss_sem = refs[-9:]
    rows, width = q_ref.shape
    temper = width ** (-0.5)
    n_late = len(bases[-1]) * own
    n_early = codes_ref.shape[0] - n_late
    late_codes_ref = codes_ref.at[pl.ds(n_early, n_late), :]
    encode(chunks, late_codes_ref, late_scales_ref)
    places = []
    for state in states:
        size = state[0].shape[0]
        places.append(pl.ds(sum(place.size for place in places), size))
        codes_ref[places[-1], :] = state[0][...]
    late_scales = late_scales_ref[...]
    ids = [ids_row(part, own) for part in bases]

    def weigh(start):
        span = pl.ds(start, block)
        spots = spot_ref[span, :]
        scores = product(q_ref[span, :], late_codes_ref[...]) * (late_scales * temper)
        late_hit = ids[-1] == spots
        late_top, late_powers, late_total, chosen = softmax_part(scores, late_hit)
        top = late_top
        for state in states:
            top = jnp.maximum(top, state[3][span, :])
        late_share = jnp.exp(late_top - top)
        shares = [jnp.exp(state[3][span, :] - top) for state in states]
        total = late_total * late_share
        for state, share in zip(states, shares):
            total += state[4][span, :] * share
            chosen += state[5][span, :]
        loss_ref[:, span] = to_row(top + jnp.log(total) - chosen)
        for state, share, place, part in zip(states, shares, places, ids):
            probs = state[2][span, :] * (share / total)
            weights = (probs - jnp.where(part == spots, 1.0, 0.0)) * state[1][...]
            weights_ref[span, place] = weights.astype(jnp.bfloat16)
        probs = late_powers * (late_share / total)
        weights = (probs - jnp.where(late_hit, 1.0, 0.0)) * late_scales
        weights_ref[span, pl.ds(n_early, n_late)] = weights.astype(jnp.bfloat16)

    starts = range(0, rows, block)
    for start in starts:
        weigh(start)
    copies = [pltpu.make_async_copy(loss_ref, loss_hbm, loss_sem)]
    copies[0].start()
    for i, start in enumerate(starts):
        span = pl.ds(start, block)
        grad = jnp.dot(weights_ref[span, :], codes_ref[...], preferred_element_type=jnp.float32)
        grad_ref[span, :] = (grad * temper).astype(jnp.bfloat16)
        copy = pltpu.make_async_copy(grad_ref.at[span, :], grad_hbm.at[span, :], sem.at[i])
        copy.start()
        copies.append(copy)
    for copy in copies:
        copy.wait()


def shards(wide, narrow, queries, documents, positives):
    own = documents.shape[0]
    rows, width = queries.shape
    f32, bf16 = jnp.float32, jnp.bfloat16
    barrier = lax.optimization_barrier
    block = min(rows, 256)
    far = range(2, wide, 2)
    evens = list(range(0, narrow, 2))
    bent_order = evens + [k ^ 1 for k in evens]
    straight_order = [k ^ (k >> 1) for k in range(narrow)]

    def swap(array, axis, bits):
        size = wide if axis == "wide" else narrow
        return lax.ppermute(array, axis, [(i, i ^ bits) for i in range(size)])

    def params(docs, kept):
        held = 6 * docs * width + 8 * rows * width + 4 * rows * (kept + 512) + 12 * block * docs
        return dict(
            compiler_params=pltpu.CompilerParams(
                vmem_limit_bytes=min(held + 4 * 2**20, 60 * 2**20)
            ),
            cost_estimate=pl.CostEstimate(flops=rows, bytes_accessed=rows, transcendentals=0),
        )

    def load(positives, queries):
        return pl.pallas_call(
            functools.partial(load_kernel, narrow, own),
            out_shape=(
                jax.ShapeDtypeStruct((rows, 1), jnp.int32),
                jax.ShapeDtypeStruct((rows, width), bf16),
            ),
            in_specs=[HBM, HBM],
            out_specs=(VMEM, VMEM),
            scratch_shapes=[pltpu.VMEM((1, rows), jnp.int32), pltpu.SemaphoreType.DMA((2,))],
            **params(0, 0),
        )(positives.reshape(1, rows), queries)

    def bases_of(distances):
        bases = []
        for k in distances:
            far_k = k - k % 2
            order = bent_order if far_k & (far_k - 1) else straight_order
            bases += [(k * narrow + n) * own for n in order]
        return bases

    def score(spots, loaded, distances, chunks):
        docs = len(distances) * own * narrow
        column = jax.ShapeDtypeStruct((rows, 1), f32)
        return pl.pallas_call(
            functools.partial(early_kernel, bases_of(distances), own, block),
            out_shape=(
                jax.ShapeDtypeStruct((docs, width), bf16),
                jax.ShapeDtypeStruct((1, docs), f32),
                jax.ShapeDtypeStruct((rows, docs), f32),
                column,
                column,
                column,
            ),
            in_specs=[VMEM] * (2 + len(chunks)),
            out_specs=(VMEM,) * 6,
            **params(docs, docs),
        )(spots, loaded, *chunks)

    shard = {0: documents} | {k: swap(documents, "narrow", k) for k in straight_order[1:]}
    base = jnp.concatenate([shard[k] for k in evens], axis=0)
    firsts = {k: swap(base, "wide", k) for k in far if k & (k - 1)}
    column = jnp.concatenate([shard[k] for k in straight_order], axis=0)
    held = {}
    for k in far:
        if k & (k - 1) == 0:
            held[k] = [swap(column, "wide", k)]
        else:
            held[k] = [firsts[k], swap(firsts[k], "narrow", 1)]
    column, positives, queries = barrier((column, positives, queries))
    spots, loaded = load(positives, queries)
    held[0] = [column]
    spots, loaded, held = barrier((spots, loaded, held))
    mine = range(0, wide, 2)
    middle = score(spots, loaded, mine, [part for k in mine for part in held[k]])
    mirrored = [swap(part, "wide", 1) for k in mine for part in held[k]]
    docs = own * narrow * wide
    bases = [bases_of(mine), bases_of([k ^ 1 for k in mine])]
    n_late = len(bases[-1]) * own
    losses, grads = pl.pallas_call(
        functools.partial(late_kernel, bases, own, block),
        out_shape=(
            jax.ShapeDtypeStruct((1, rows), f32),
            jax.ShapeDtypeStruct((rows, width), bf16),
        ),
        in_specs=[VMEM] * (2 + len(middle) + len(mirrored)),
        out_specs=(HBM, HBM),
        scratch_shapes=[
            pltpu.VMEM((docs, width), bf16),
            pltpu.VMEM((1, n_late), f32),
            pltpu.VMEM((rows, docs), bf16),
            pltpu.VMEM((1, rows), f32),
            pltpu.VMEM((rows, width), bf16),
            pltpu.SemaphoreType.DMA((rows // block,)),
            pltpu.SemaphoreType.DMA(()),
        ],
        **params(docs, docs),
    )(spots, loaded, *middle, *mirrored)
    return losses.reshape(rows), grads


def solution(mesh):
    wide, narrow = mesh.shape["wide"], mesh.shape["narrow"]
    rows = P(AXES, None)
    return jax.shard_map(
        functools.partial(shards, wide, narrow),
        mesh=mesh,
        in_specs=(rows, rows, P(AXES)),
        out_specs=(P(AXES), rows),
        check_vma=False,
    )
```

```python
import functools

import jax
import jax.numpy as jnp
from jax import lax
from jax.experimental import pallas as pl
from jax.experimental.pallas import tpu as pltpu
from jax.sharding import PartitionSpec as P

AXES = ("wide", "narrow")
NT = (((1,), (1,)), ((), ()))
VMEM = pl.BlockSpec(memory_space=pltpu.VMEM)
HBM = pl.BlockSpec(memory_space=pltpu.HBM)


def to_row(column):
    parts = []
    for start in range(0, column.shape[0], 128):
        piece = column[start : start + 128]
        size = piece.shape[0]
        r = lax.broadcasted_iota(jnp.int32, (size, size), 0)
        c = lax.broadcasted_iota(jnp.int32, (size, size), 1)
        parts.append(jnp.sum(jnp.where(r == c, piece, 0), axis=0, keepdims=True))
    return parts[0] if len(parts) == 1 else jnp.concatenate(parts, axis=1)


def encode(chunks, codes_ref, scales_ref):
    group, start = [], 0
    for chunk in chunks:
        group.append(chunk[...].astype(jnp.float32))
        size = sum(part.shape[0] for part in group)
        if size % 128 and chunk is not chunks[-1]:
            continue
        values = group[0] if len(group) == 1 else jnp.concatenate(group, axis=0)
        scale = jnp.max(jnp.abs(values), axis=1, keepdims=True) + 1e-06
        codes_ref[pl.ds(start, size), :] = (values / scale).astype(jnp.bfloat16)
        scales_ref[:, pl.ds(start, size)] = to_row(scale)
        group, start = [], start + size


def ids_row(bases, own):
    rows = []
    size = max(own, 128)
    lane = lax.broadcasted_iota(jnp.int32, (1, size), 1)
    for start in range(0, len(bases), size // own):
        group = bases[start : start + size // own]
        shift = jnp.full((1, size), group[0], jnp.int32)
        for i, base in enumerate(group[1:], 1):
            shift = jnp.where(lane >= i * own, base - i * own, shift)
        rows.append((lane + shift)[:, : len(group) * own])
    return rows[0] if len(rows) == 1 else jnp.concatenate(rows, axis=1)


def softmax_part(scores, hit):
    top = jnp.max(scores, axis=1, keepdims=True)
    powers = jnp.exp(scores - top)
    total = jnp.sum(powers, axis=1, keepdims=True)
    chosen = jnp.sum(jnp.where(hit, scores, 0.0), axis=1, keepdims=True)
    return top, powers, total, chosen


def product(q, codes):
    return lax.dot_general(q, codes, NT, preferred_element_type=jnp.float32)


def load_kernel(narrow, own, positives_hbm, queries_hbm, *refs):
    parts, (spot_ref, q_ref, packed_ref, positives_ref, sem) = refs[:-5], refs[-5:]
    fetch = pltpu.make_async_copy(positives_hbm, positives_ref, sem.at[0])
    fetch.start()
    copy = pltpu.make_async_copy(queries_hbm, q_ref, sem.at[1])
    copy.start()
    start = 0
    for part in parts:
        packed_ref[pl.ds(start, part.shape[0]), :] = part[...]
        start += part.shape[0]
    fetch.wait()
    me = lax.axis_index("wide") * narrow + lax.axis_index("narrow")
    local = (positives_ref[...] ^ (me * own)).astype(jnp.float32)
    for start in range(0, local.shape[1], 128):
        piece = local[:, start : start + 128]
        size = piece.shape[1]
        r = lax.broadcasted_iota(jnp.int32, (size, size), 0)
        c = lax.broadcasted_iota(jnp.int32, (size, size), 1)
        spot = jnp.sum(jnp.where(r == c, piece, 0.0), axis=1, keepdims=True)
        spot_ref[pl.ds(start, size), :] = spot.astype(jnp.int32)
    copy.wait()


def early_kernel(bases, own, block, spot_ref, q_ref, *refs):
    chunks = refs[:-6]
    codes_ref, scales_ref, powers_ref, top_ref, total_ref, chosen_ref = refs[-6:]
    rows, width = q_ref.shape
    temper = width ** (-0.5)
    encode(chunks, codes_ref, scales_ref)
    ids = ids_row(bases, own)
    for start in range(0, rows, block):
        span = pl.ds(start, block)
        scores = product(q_ref[span, :], codes_ref[...]) * (scales_ref[...] * temper)
        top, powers, total, chosen = softmax_part(scores, ids == spot_ref[span, :])
        powers_ref[span, :] = powers
        top_ref[span, :] = top
        total_ref[span, :] = total
        chosen_ref[span, :] = chosen


def late_kernel(bases, own, block, spot_ref, q_ref, *refs):
    states = [refs[6 * i : 6 * i + 6] for i in range(len(bases) - 1)]
    chunks = refs[6 * len(states) : -9]
    loss_hbm, grad_hbm, codes_ref, late_scales_ref, weights_ref, loss_ref, grad_ref, sem, loss_sem = refs[-9:]
    rows, width = q_ref.shape
    temper = width ** (-0.5)
    n_late = len(bases[-1]) * own
    n_early = codes_ref.shape[0] - n_late
    late_codes_ref = codes_ref.at[pl.ds(n_early, n_late), :]
    encode(chunks, late_codes_ref, late_scales_ref)
    places = []
    for state in states:
        size = state[0].shape[0]
        places.append(pl.ds(sum(place.size for place in places), size))
        codes_ref[places[-1], :] = state[0][...]
    late_scales = late_scales_ref[...]
    ids = [ids_row(part, own) for part in bases]

    def weigh(start):
        span = pl.ds(start, block)
        spots = spot_ref[span, :]
        scores = product(q_ref[span, :], late_codes_ref[...]) * (late_scales * temper)
        late_hit = ids[-1] == spots
        late_top, late_powers, late_total, chosen = softmax_part(scores, late_hit)
        top = late_top
        for state in states:
            top = jnp.maximum(top, state[3][span, :])
        late_share = jnp.exp(late_top - top)
        shares = [jnp.exp(state[3][span, :] - top) for state in states]
        total = late_total * late_share
        for state, share in zip(states, shares):
            total += state[4][span, :] * share
            chosen += state[5][span, :]
        loss_ref[:, span] = to_row(top + jnp.log(total) - chosen)
        for state, share, place, part in zip(states, shares, places, ids):
            probs = state[2][span, :] * (share / total)
            weights = (probs - jnp.where(part == spots, 1.0, 0.0)) * state[1][...]
            weights_ref[span, place] = weights.astype(jnp.bfloat16)
        probs = late_powers * (late_share / total)
        weights = (probs - jnp.where(late_hit, 1.0, 0.0)) * late_scales
        weights_ref[span, pl.ds(n_early, n_late)] = weights.astype(jnp.bfloat16)

    starts = range(0, rows, block)
    for start in starts:
        weigh(start)
    copies = [pltpu.make_async_copy(loss_ref, loss_hbm, loss_sem)]
    copies[0].start()
    for i, start in enumerate(starts):
        span = pl.ds(start, block)
        grad = jnp.dot(weights_ref[span, :], codes_ref[...], preferred_element_type=jnp.float32)
        grad_ref[span, :] = (grad * temper).astype(jnp.bfloat16)
        copy = pltpu.make_async_copy(grad_ref.at[span, :], grad_hbm.at[span, :], sem.at[i])
        copy.start()
        copies.append(copy)
    for copy in copies:
        copy.wait()


def shards(wide, narrow, queries, documents, positives):
    own = documents.shape[0]
    rows, width = queries.shape
    f32, bf16 = jnp.float32, jnp.bfloat16
    barrier = lax.optimization_barrier
    block = min(rows, 256)
    far = range(2, wide, 2)
    evens = list(range(0, narrow, 2))
    straight_order = [k ^ (k >> 1) for k in range(narrow)]

    def swap(chunk, bits, step=0):
        array, places = chunk
        jump = bits * narrow + step
        pairs = [(i, i ^ jump) for i in range(wide * narrow)]
        return lax.ppermute(array, AXES, pairs), [place ^ jump for place in places]

    def join(chunks):
        return jnp.concatenate([c[0] for c in chunks], axis=0), [p for c in chunks for p in c[1]]

    def params(docs, kept):
        held = 6 * docs * width + 8 * rows * width + 4 * rows * (kept + 512) + 12 * block * docs
        return dict(
            compiler_params=pltpu.CompilerParams(
                vmem_limit_bytes=min(held + 4 * 2**20, 60 * 2**20)
            ),
            cost_estimate=pl.CostEstimate(flops=rows, bytes_accessed=rows, transcendentals=0),
        )

    def load(positives, queries, parts):
        return pl.pallas_call(
            functools.partial(load_kernel, narrow, own),
            out_shape=(
                jax.ShapeDtypeStruct((rows, 1), jnp.int32),
                jax.ShapeDtypeStruct((rows, width), bf16),
                jax.ShapeDtypeStruct((sum(part.shape[0] for part in parts), width), bf16),
            ),
            in_specs=[HBM, HBM] + [VMEM] * len(parts),
            out_specs=(VMEM, VMEM, VMEM),
            scratch_shapes=[pltpu.VMEM((1, rows), jnp.int32), pltpu.SemaphoreType.DMA((2,))],
            **params(own * narrow * wide // 2, 0),
        )(positives.reshape(1, rows), queries, *parts)

    def bases_of(chunks):
        return [place * own for _, places in chunks for place in places]

    def score(spots, loaded, chunks):
        bases = bases_of(chunks)
        docs = len(bases) * own
        column = jax.ShapeDtypeStruct((rows, 1), f32)
        return pl.pallas_call(
            functools.partial(early_kernel, bases, own, block),
            out_shape=(
                jax.ShapeDtypeStruct((docs, width), bf16),
                jax.ShapeDtypeStruct((1, docs), f32),
                jax.ShapeDtypeStruct((rows, docs), f32),
                column,
                column,
                column,
            ),
            in_specs=[VMEM] * (2 + len(chunks)),
            out_specs=(VMEM,) * 6,
            **params(docs, docs),
        )(spots, loaded, *[array for array, _ in chunks])

    shard = {0: (documents, [0])}
    for k in straight_order[1:]:
        shard[k] = swap(shard[0], 0, k)
    base = join([shard[k] for k in evens])
    firsts = [swap(base, k ^ 0) for k in far if k & (k - 1)]
    column = join([shard[k] for k in straight_order])
    chunks = [swap(column, k ^ 1) for k in far if k & (k - 1) == 0]
    chunks += [swap(first, 1, 1) for first in firsts]
    parts, positives, queries = barrier(([c[0] for c in [column] + firsts], positives, queries))
    spots, loaded, packed = load(positives, queries, parts)
    chunks = [(packed, [p for c in [column] + firsts for p in c[1]])] + chunks
    spots, loaded, arrays = barrier((spots, loaded, [array for array, _ in chunks]))
    chunks = [(array, places) for array, (_, places) in zip(arrays, chunks)]
    middle = score(spots, loaded, chunks)
    mirrored = [swap(chunk, 1) for chunk in chunks]
    docs = own * narrow * wide
    bases = [bases_of(chunks), bases_of(mirrored)]
    n_late = len(bases[-1]) * own
    losses, grads = pl.pallas_call(
        functools.partial(late_kernel, bases, own, block),
        out_shape=(
            jax.ShapeDtypeStruct((1, rows), f32),
            jax.ShapeDtypeStruct((rows, width), bf16),
        ),
        in_specs=[VMEM] * (2 + len(middle) + len(mirrored)),
        out_specs=(HBM, HBM),
        scratch_shapes=[
            pltpu.VMEM((docs, width), bf16),
            pltpu.VMEM((1, n_late), f32),
            pltpu.VMEM((rows, docs), bf16),
            pltpu.VMEM((1, rows), f32),
            pltpu.VMEM((rows, width), bf16),
            pltpu.SemaphoreType.DMA((rows // block,)),
            pltpu.SemaphoreType.DMA(()),
        ],
        **params(docs, docs),
    )(spots, loaded, *middle, *[array for array, _ in mirrored])
    return losses.reshape(rows), grads


def solution(mesh):
    wide, narrow = mesh.shape["wide"], mesh.shape["narrow"]
    rows = P(AXES, None)
    return jax.shard_map(
        functools.partial(shards, wide, narrow),
        mesh=mesh,
        in_specs=(rows, rows, P(AXES)),
        out_specs=(P(AXES), rows),
        check_vma=False,
    )
```

```python
import functools

import jax
import jax.numpy as jnp
from jax import lax
from jax.experimental import pallas as pl
from jax.experimental.pallas import tpu as pltpu
from jax.sharding import PartitionSpec as P

AXES = ("wide", "narrow")
NT = (((1,), (1,)), ((), ()))
VMEM = pl.BlockSpec(memory_space=pltpu.VMEM)
HBM = pl.BlockSpec(memory_space=pltpu.HBM)


def to_row(column):
    parts = []
    for start in range(0, column.shape[0], 128):
        piece = column[start : start + 128]
        size = piece.shape[0]
        r = lax.broadcasted_iota(jnp.int32, (size, size), 0)
        c = lax.broadcasted_iota(jnp.int32, (size, size), 1)
        parts.append(jnp.sum(jnp.where(r == c, piece, 0), axis=0, keepdims=True))
    return parts[0] if len(parts) == 1 else jnp.concatenate(parts, axis=1)


def encode(chunks, codes_ref, scales_ref):
    group, start = [], 0
    for chunk in chunks:
        group.append(chunk[...].astype(jnp.float32))
        size = sum(part.shape[0] for part in group)
        if size % 128 and chunk is not chunks[-1]:
            continue
        values = group[0] if len(group) == 1 else jnp.concatenate(group, axis=0)
        scale = jnp.max(jnp.abs(values), axis=1, keepdims=True) + 1e-06
        codes_ref[pl.ds(start, size), :] = (values / scale).astype(jnp.bfloat16)
        scales_ref[:, pl.ds(start, size)] = to_row(scale)
        group, start = [], start + size


def ids_row(bases, own):
    rows = []
    size = max(own, 128)
    lane = lax.broadcasted_iota(jnp.int32, (1, size), 1)
    for start in range(0, len(bases), size // own):
        group = bases[start : start + size // own]
        shift = jnp.full((1, size), group[0], jnp.int32)
        for i, base in enumerate(group[1:], 1):
            shift = jnp.where(lane >= i * own, base - i * own, shift)
        rows.append((lane + shift)[:, : len(group) * own])
    return rows[0] if len(rows) == 1 else jnp.concatenate(rows, axis=1)


def softmax_part(scores, hit):
    top = jnp.max(scores, axis=1, keepdims=True)
    powers = jnp.exp(scores - top)
    total = jnp.sum(powers, axis=1, keepdims=True)
    chosen = jnp.sum(jnp.where(hit, scores, 0.0), axis=1, keepdims=True)
    return top, powers, total, chosen


def product(q, codes):
    return lax.dot_general(q, codes, NT, preferred_element_type=jnp.float32)


def load_kernel(narrow, own, positives_hbm, queries_hbm, *refs):
    parts, (spot_ref, q_ref, packed_ref, positives_ref, sem) = refs[:-5], refs[-5:]
    fetch = pltpu.make_async_copy(positives_hbm, positives_ref, sem.at[0])
    fetch.start()
    copy = pltpu.make_async_copy(queries_hbm, q_ref, sem.at[1])
    copy.start()
    start = 0
    for part in parts:
        packed_ref[pl.ds(start, part.shape[0]), :] = part[...]
        start += part.shape[0]
    fetch.wait()
    me = lax.axis_index("wide") * narrow + lax.axis_index("narrow")
    local = (positives_ref[...] ^ (me * own)).astype(jnp.float32)
    for start in range(0, local.shape[1], 128):
        piece = local[:, start : start + 128]
        size = piece.shape[1]
        r = lax.broadcasted_iota(jnp.int32, (size, size), 0)
        c = lax.broadcasted_iota(jnp.int32, (size, size), 1)
        spot = jnp.sum(jnp.where(r == c, piece, 0.0), axis=1, keepdims=True)
        spot_ref[pl.ds(start, size), :] = spot.astype(jnp.int32)
    copy.wait()


def early_kernel(bases, own, block, spot_ref, q_ref, *refs):
    chunks = refs[:-6]
    codes_ref, scales_ref, powers_ref, top_ref, total_ref, chosen_ref = refs[-6:]
    rows, width = q_ref.shape
    temper = width ** (-0.5)
    encode(chunks, codes_ref, scales_ref)
    ids = ids_row(bases, own)
    for start in range(0, rows, block):
        span = pl.ds(start, block)
        scores = product(q_ref[span, :], codes_ref[...]) * (scales_ref[...] * temper)
        top, powers, total, chosen = softmax_part(scores, ids == spot_ref[span, :])
        powers_ref[span, :] = powers
        top_ref[span, :] = top
        total_ref[span, :] = total
        chosen_ref[span, :] = chosen


def late_kernel(bases, own, block, spot_ref, q_ref, *refs):
    states = [refs[6 * i : 6 * i + 6] for i in range(len(bases) - 1)]
    chunks = refs[6 * len(states) : -9]
    loss_hbm, grad_hbm, codes_ref, late_scales_ref, weights_ref, loss_ref, grad_ref, sem, loss_sem = refs[-9:]
    rows, width = q_ref.shape
    temper = width ** (-0.5)
    n_late = len(bases[-1]) * own
    n_early = codes_ref.shape[0] - n_late
    late_codes_ref = codes_ref.at[pl.ds(n_early, n_late), :]
    encode(chunks, late_codes_ref, late_scales_ref)
    places = []
    for state in states:
        size = state[0].shape[0]
        places.append(pl.ds(sum(place.size for place in places), size))
        codes_ref[places[-1], :] = state[0][...]
    late_scales = late_scales_ref[...]
    ids = [ids_row(part, own) for part in bases]

    def weigh(start):
        span = pl.ds(start, block)
        spots = spot_ref[span, :]
        scores = product(q_ref[span, :], late_codes_ref[...]) * (late_scales * temper)
        late_hit = ids[-1] == spots
        late_top, late_powers, late_total, chosen = softmax_part(scores, late_hit)
        top = late_top
        for state in states:
            top = jnp.maximum(top, state[3][span, :])
        late_share = jnp.exp(late_top - top)
        shares = [jnp.exp(state[3][span, :] - top) for state in states]
        total = late_total * late_share
        for state, share in zip(states, shares):
            total += state[4][span, :] * share
            chosen += state[5][span, :]
        loss_ref[:, span] = to_row(top + jnp.log(total) - chosen)
        for state, share, place, part in zip(states, shares, places, ids):
            probs = state[2][span, :] * (share / total)
            weights = (probs - jnp.where(part == spots, 1.0, 0.0)) * state[1][...]
            weights_ref[span, place] = weights.astype(jnp.bfloat16)
        probs = late_powers * (late_share / total)
        weights = (probs - jnp.where(late_hit, 1.0, 0.0)) * late_scales
        weights_ref[span, pl.ds(n_early, n_late)] = weights.astype(jnp.bfloat16)

    starts = range(0, rows, block)
    for start in starts:
        weigh(start)
    copies = [pltpu.make_async_copy(loss_ref, loss_hbm, loss_sem)]
    copies[0].start()
    for i, start in enumerate(starts):
        span = pl.ds(start, block)
        grad = jnp.dot(weights_ref[span, :], codes_ref[...], preferred_element_type=jnp.float32)
        grad_ref[span, :] = (grad * temper).astype(jnp.bfloat16)
        copy = pltpu.make_async_copy(grad_ref.at[span, :], grad_hbm.at[span, :], sem.at[i])
        copy.start()
        copies.append(copy)
    for copy in copies:
        copy.wait()


def shards(wide, narrow, queries, documents, positives):
    own = documents.shape[0]
    rows, width = queries.shape
    f32, bf16 = jnp.float32, jnp.bfloat16
    barrier = lax.optimization_barrier
    block = min(rows, 256)
    far = range(2, wide, 2)
    evens = list(range(0, narrow, 2))
    straight_order = [k ^ (k >> 1) for k in range(narrow)]

    def swap(chunk, bits, step=0):
        array, places = chunk
        jump = bits * narrow + step
        pairs = [(i, i ^ jump) for i in range(wide * narrow)]
        return lax.ppermute(array, AXES, pairs), [place ^ jump for place in places]

    def join(chunks):
        return jnp.concatenate([c[0] for c in chunks], axis=0), [p for c in chunks for p in c[1]]

    def params(docs, kept):
        held = 6 * docs * width + 8 * rows * width + 4 * rows * (kept + 512) + 12 * block * docs
        return dict(
            compiler_params=pltpu.CompilerParams(
                vmem_limit_bytes=min(held + 4 * 2**20, 60 * 2**20)
            ),
            cost_estimate=pl.CostEstimate(flops=rows, bytes_accessed=rows, transcendentals=0),
        )

    def load(positives, queries, parts):
        return pl.pallas_call(
            functools.partial(load_kernel, narrow, own),
            out_shape=(
                jax.ShapeDtypeStruct((rows, 1), jnp.int32),
                jax.ShapeDtypeStruct((rows, width), bf16),
                jax.ShapeDtypeStruct((sum(part.shape[0] for part in parts), width), bf16),
            ),
            in_specs=[HBM, HBM] + [VMEM] * len(parts),
            out_specs=(VMEM, VMEM, VMEM),
            scratch_shapes=[pltpu.VMEM((1, rows), jnp.int32), pltpu.SemaphoreType.DMA((2,))],
            **params(own * narrow * wide // 2, 0),
        )(positives.reshape(1, rows), queries, *parts)

    def bases_of(chunks):
        return [place * own for _, places in chunks for place in places]

    def score(spots, loaded, chunks):
        bases = bases_of(chunks)
        docs = len(bases) * own
        column = jax.ShapeDtypeStruct((rows, 1), f32)
        return pl.pallas_call(
            functools.partial(early_kernel, bases, own, block),
            out_shape=(
                jax.ShapeDtypeStruct((docs, width), bf16),
                jax.ShapeDtypeStruct((1, docs), f32),
                jax.ShapeDtypeStruct((rows, docs), f32),
                column,
                column,
                column,
            ),
            in_specs=[VMEM] * (2 + len(chunks)),
            out_specs=(VMEM,) * 6,
            **params(docs, docs),
        )(spots, loaded, *[array for array, _ in chunks])

    shard = {0: (documents, [0])}
    for k in straight_order[1:]:
        shard[k] = swap(shard[0], 0, k)
    base = join([shard[k] for k in evens])
    firsts = [swap(base, k ^ 0) for k in far if k & (k - 1)]
    column = join([shard[k] for k in straight_order])
    chunks = [swap(column, k ^ 1) for k in far if k & (k - 1) == 0]
    chunks += [swap(first, 1, 1) for first in firsts]
    parts, positives, queries = barrier(([c[0] for c in [column] + firsts], positives, queries))
    spots, loaded, packed = load(positives, queries, parts)
    chunks = [(packed, [p for c in [column] + firsts for p in c[1]])] + chunks
    early, early_places = swap(chunks[0], 1)
    spots, loaded, arrays = barrier((spots, loaded, [array for array, _ in chunks]))
    chunks = [(array, places) for array, (_, places) in zip(arrays, chunks)]
    middle = score(spots, loaded, chunks)
    mirrored = [(early, early_places)] + [swap(chunk, 1) for chunk in chunks[1:]]
    docs = own * narrow * wide
    bases = [bases_of(chunks), bases_of(mirrored)]
    n_late = len(bases[-1]) * own
    losses, grads = pl.pallas_call(
        functools.partial(late_kernel, bases, own, block),
        out_shape=(
            jax.ShapeDtypeStruct((1, rows), f32),
            jax.ShapeDtypeStruct((rows, width), bf16),
        ),
        in_specs=[VMEM] * (2 + len(middle) + len(mirrored)),
        out_specs=(HBM, HBM),
        scratch_shapes=[
            pltpu.VMEM((docs, width), bf16),
            pltpu.VMEM((1, n_late), f32),
            pltpu.VMEM((rows, docs), bf16),
            pltpu.VMEM((1, rows), f32),
            pltpu.VMEM((rows, width), bf16),
            pltpu.SemaphoreType.DMA((rows // block,)),
            pltpu.SemaphoreType.DMA(()),
        ],
        **params(docs, docs),
    )(spots, loaded, *middle, *[array for array, _ in mirrored])
    return losses.reshape(rows), grads


def solution(mesh):
    wide, narrow = mesh.shape["wide"], mesh.shape["narrow"]
    rows = P(AXES, None)
    return jax.shard_map(
        functools.partial(shards, wide, narrow),
        mesh=mesh,
        in_specs=(rows, rows, P(AXES)),
        out_specs=(P(AXES), rows),
        check_vma=False,
    )
```
